32 devices in a mesh: chan: 16 (over z, y, core), tm: 2 (over x).
Axes of the slice: x: 2, y: 2, z: 4, core: 2. Of those that a mesh axis runs over, the one named last changes fastest.
Arguments:
- raw_samples: bfloat16 [64, 12288], P('tm', 'chan'), may hold values from -6 to 6
- channel_order: int32 [12288], P('chan'), may hold values from 0 to 12287, as said below
- conv_weight: bfloat16 [32, 81], replicated, may hold values from -0.625 to 0.625
- conv_bias: float32 [32], replicated, may hold values from -3 to 3
- taps: bfloat16 [255], replicated, may hold values from -1.5 to 1.5
- shifts: int32 [16, 255], replicated, may hold values from -8 to 8, as said below
Outputs:
- coherence: float32 [16, 32, 6144], P(None, 'tm', 'chan')
The draws below stay inside these ranges and needn't reach their ends.
Inputs may be any that keep to these rules, and one draw needn't show every extreme that they name: shifts[v, j] = floor((j - 127) * k_v / 127) for an integer slowness k_v of velocity v between -8 and 8; one velocity has k_v = 8 and another k_v = -8. `channel_order`: a permutation that keeps each channel inside its aligned block of 768 channels.
All inputs are finite; a program needn't handle non-finite values.
Results may differ from the reference program's by a relative error of at most 0.0028.
Values may be sent and summed in bfloat16 or wider, within the bound.
A program may use at most 64 MiB of HBM per device.

```python
import jax
import jax.numpy as jnp
from jax import lax

F = 32
VEL = 16
TAPS = 255
KS = 9
SMAX = 8
CE = 384
HALF = 127
CHANS = 6144
TIMES = 32
CH_RAW = 12288
T_RAW = 64


def draw_shifts(key, part):
    speeds = jax.random.randint(jax.random.fold_in(key, 1), (VEL,), -SMAX, SMAX + 1)
    picked = jax.random.permutation(jax.random.fold_in(key, 2), VEL)
    speeds = speeds.at[picked[0]].set(SMAX).at[picked[1]].set(-SMAX)
    offsets = jnp.arange(TAPS, dtype=jnp.int32) - HALF
    return (offsets[None, :] * speeds[:, None] // HALF).astype(jnp.int32)


def draw_channel_order(key, part):
    blocks = CH_RAW // (2 * CE)
    keys_all = jax.random.split(jax.random.fold_in(key, 3), blocks)
    orders = jax.vmap(lambda one_key: jax.random.permutation(one_key, 2 * CE))(keys_all)
    starts = (jnp.arange(blocks) * 2 * CE)[:, None]
    return (orders + starts).reshape(-1).astype(jnp.int32)


def block_scale(stream_key, extent, shards, smallest, high):
    def one(axis_at, shards_of):
        heights = jax.random.uniform(jax.random.fold_in(jax.random.fold_in(stream_key, 6), axis_at), (shards_of,), jnp.float32, smallest / len(shards), high / len(shards))
        return jnp.repeat(jnp.exp(heights), extent[axis_at] // shards_of).reshape((-1,) + (1,) * (len(extent) - axis_at - 1))

    factor_of = one(*shards[0])
    for cut in shards[1:]:
        factor_of = factor_of * one(*cut)
    return factor_of


def scatter_about(key, extent, spread, most, shards=(), kind=jnp.bfloat16):
    factor_of = block_scale(key, extent, shards, -0.22, 0.18) if shards else 1.0
    result = jax.random.normal(key, extent, jnp.float32) * spread * factor_of
    return jnp.minimum(jnp.maximum(result, -most), most).astype(kind)


def setup_inputs(seed: int = 0) -> dict:
    keys = jax.random.split(jax.random.key(seed), 7)
    return {
        "raw_samples": scatter_about(keys[0], (T_RAW, CH_RAW), 1.0, 6.0, ((0, 2), (1, 16))),
        "channel_order": draw_channel_order(jax.random.fold_in(keys[6], 71), 0),
        "conv_weight": scatter_about(keys[2], (F, KS * KS), (KS * KS) ** -0.5, 0.625),
        "conv_bias": scatter_about(keys[3], (F,), 0.5, 3.0, (), jnp.float32),
        "taps": scatter_about(keys[4], (TAPS,), 0.25, 1.5),
        "shifts": draw_shifts(jax.random.fold_in(keys[6], 71), 0),
    }


def encode(ordered, conv_weight, conv_bias):
    margin = KS // 2
    padded = jnp.pad(ordered, margin)
    out_times = ordered.shape[0] // 2
    out_chans = ordered.shape[1] // 2
    pieces = [padded[row_off:row_off + 2 * out_times:2, col_off:col_off + 2 * out_chans:2]
              for row_off in range(KS) for col_off in range(KS)]
    patches = jnp.stack(pieces).reshape(KS * KS, out_times * out_chans)
    summed = jnp.dot(conv_weight, patches, preferred_element_type=jnp.float32) + conv_bias[:, None]
    return jnp.tanh(summed).astype(jnp.bfloat16).reshape(-1, out_times, out_chans)


def diagonal_band(products, width):
    outer, rows_count, cols_count = products.shape
    flattened = products.reshape(outer, rows_count * cols_count)
    flattened = jnp.pad(flattened, ((0, 0), (0, rows_count)))
    return flattened.reshape(outer, rows_count, cols_count + 1)[:, :, :width]


def lag_weights(taps, shifts):
    lag_values = jnp.arange(2 * SMAX + 1, dtype=jnp.int32) - SMAX
    matches = shifts[None, :, :] == lag_values[:, None, None]
    return jnp.where(matches, taps.astype(jnp.float32)[None, None, :], jnp.float32(0.0))


def reference(raw_samples, channel_order, conv_weight, conv_bias, taps, shifts):
    ordered = jnp.take(raw_samples, channel_order, axis=1)
    features = encode(ordered, conv_weight, conv_bias)
    padded = jnp.pad(features, ((0, 0), (SMAX, SMAX), (HALF, HALF)))
    lag_table = lag_weights(taps, shifts)
    zero_index = jnp.zeros((), jnp.int32)

    def one_block(offset):
        offset = offset.astype(jnp.int32)
        own_rows = lax.dynamic_slice(features, (zero_index, zero_index, offset), (F, TIMES, CE)).astype(jnp.float32)
        partners = lax.dynamic_slice(padded, (zero_index, zero_index, offset), (F, TIMES + 2 * SMAX, CE + 2 * HALF))

        def add_lag(lag_index, running):
            lag_index = lag_index.astype(jnp.int32)
            shifted = lax.dynamic_slice_in_dim(partners, lag_index, TIMES, 1).astype(jnp.float32)
            products = (jnp.einsum('ftc,fte->tce', own_rows, shifted) * (1.0 / F)).astype(jnp.bfloat16)
            banded = diagonal_band(products, TAPS).astype(jnp.float32)
            weights = lax.dynamic_index_in_dim(lag_table, lag_index, 0, keepdims=False)
            return running + jnp.einsum('vj,tcj->vtc', weights, banded)

        return lax.fori_loop(jnp.int32(0), jnp.int32(2 * SMAX + 1), add_lag,
                             jnp.zeros((VEL, TIMES, CE), jnp.float32))

    offsets = (jnp.arange(CHANS // CE, dtype=jnp.int32) * CE).astype(jnp.int32)
    blocks_out = lax.map(one_block, offsets)
    return jnp.transpose(blocks_out, (1, 2, 0, 3)).reshape(VEL, TIMES, CHANS)
```

```python
import jax
import jax.numpy as jnp
from jax import lax
from jax.experimental import pallas as pl
from jax.experimental.pallas import tpu as pltpu
from jax.sharding import PartitionSpec as P

F = 32
TAPS = 255
KS = 9
SMAX = 8
HALF = 127
BLOCK = 128


def extended_2(value, sides, width):
    for axis, dim in sides:
        devices, length = (lax.axis_size(axis), value.shape[dim])
        up = [(i, (i + 1) % devices) for i in range(devices - 1)]
        down = [(j, i) for i, j in up]
        last = lax.slice_in_dim(value, length - width, length, axis=dim)
        first = lax.slice_in_dim(value, 0, width, axis=dim)
        before = lax.ppermute(last, axis, up)
        after = lax.ppermute(first, axis, down)
        value = jnp.concatenate([before, value, after], axis=dim)
    return value


def lag_weights(taps, shifts):
    rev_taps = jnp.pad(taps[::-1], (1, 0))
    rev_shifts = jnp.pad(shifts.T[::-1], ((1, 0), (0, 0)))
    lag_values = jnp.arange(2 * SMAX + 1, dtype=jnp.int32) - SMAX
    matches = rev_shifts[None, :, :] == lag_values[:, None, None]
    return jnp.where(matches, rev_taps[None, :, None], jnp.zeros((), jnp.bfloat16))


def correlate_kernel(own_ref, ext_ref, weight_ref, out_ref):
    time = pl.program_id(0)
    chans = own_ref.shape[2]
    blocks = chans // BLOCK
    for block in range(blocks):
        own = own_ref[0, :, block * BLOCK : (block + 1) * BLOCK]
        own = (own.astype(jnp.float32) * (1.0 / F)).T.astype(jnp.bfloat16)
        start = (blocks - 1 - block) * BLOCK
        total = jnp.zeros((BLOCK, weight_ref.shape[2]), jnp.float32)
        for lag in range(2 * SMAX + 1):
            partner = ext_ref[time + lag, :, start : start + 3 * BLOCK]
            products = jnp.dot(own, partner, preferred_element_type=jnp.float32)
            skewed = pltpu.roll(products, 0, 1, stride=1, stride_axis=0)
            banded = skewed[:, BLOCK:].astype(jnp.bfloat16)
            total += jnp.dot(banded, weight_ref[lag], preferred_element_type=jnp.float32)
        out_ref[0, :, block * BLOCK : (block + 1) * BLOCK] = total.T


def encode_region(padded, out_times, out_chans, conv_weight, conv_bias):
    pieces = [
        padded[row_off : row_off + 2 * out_times : 2, col_off : col_off + 2 * out_chans : 2]
        for row_off in range(KS)
        for col_off in range(KS)
    ]
    patches = jnp.stack(pieces).reshape(KS * KS, out_times * out_chans)
    summed = jnp.dot(conv_weight, patches, preferred_element_type=jnp.float32) + conv_bias[:, None]
    return jnp.tanh(summed).astype(jnp.bfloat16).reshape(-1, out_times, out_chans)


def body(raw_samples, channel_order, conv_weight, conv_bias, taps, shifts):
    local_times = raw_samples.shape[0] // 2
    local_chans = raw_samples.shape[1] // 2
    local_index = channel_order - lax.axis_index("chan") * raw_samples.shape[1]
    ordered = jnp.take(raw_samples, local_index, axis=1)
    padded = extended_2(ordered, (("chan", 1), ("tm", 0)), KS // 2)
    features = encode_region(padded, local_times, local_chans, conv_weight, conv_bias)
    features = features.transpose(1, 0, 2)
    extended = extended_2(features, (("chan", 2),), HALF)
    extended = extended_2(extended, (("tm", 0),), SMAX)
    extended = jnp.pad(extended, ((0, 0), (0, 0), (0, 2)))[:, :, ::-1]
    weights = lag_weights(taps, shifts)
    vel_count = shifts.shape[0]
    summed = pl.pallas_call(
        correlate_kernel,
        grid=(local_times,),
        in_specs=[
            pl.BlockSpec((1, F, local_chans), lambda t: (t, 0, 0)),
            pl.BlockSpec(extended.shape, lambda t: (0, 0, 0)),
            pl.BlockSpec(weights.shape, lambda t: (0, 0, 0)),
        ],
        out_specs=pl.BlockSpec((1, vel_count, local_chans), lambda t: (t, 0, 0)),
        out_shape=jax.ShapeDtypeStruct((local_times, vel_count, local_chans), jnp.float32),
        compiler_params=pltpu.CompilerParams(vmem_limit_bytes=40 * 1024 * 1024),
    )(features, extended, weights)
    return summed.transpose(1, 0, 2)


def solution(mesh):
    placed = (P("tm", "chan"), P("chan"), P(), P(), P(), P())
    return jax.shard_map(
        body, mesh=mesh, in_specs=placed, out_specs=P(None, "tm", "chan"), check_vma=False
    )
```

```python
import jax
import jax.numpy as jnp
from jax import lax
from jax.experimental import pallas as pl
from jax.experimental.pallas import tpu as pltpu
from jax.sharding import PartitionSpec as P

F = 32
TAPS = 255
KS = 9
SMAX = 8
HALF = 127
BLOCK = 128


def extended_2(value, sides, width):
    for axis, dim in sides:
        devices, length = (lax.axis_size(axis), value.shape[dim])
        up = [(i, (i + 1) % devices) for i in range(devices - 1)]
        down = [(j, i) for i, j in up]
        last = lax.slice_in_dim(value, length - width, length, axis=dim)
        first = lax.slice_in_dim(value, 0, width, axis=dim)
        before = lax.ppermute(last, axis, up)
        after = lax.ppermute(first, axis, down)
        value = jnp.concatenate([before, value, after], axis=dim)
    return value


def lag_weights(taps, shifts):
    rev_taps = jnp.pad(taps[::-1], (1, 0))
    rev_shifts = jnp.pad(shifts.T[::-1], ((1, 0), (0, 0)))
    lag_values = jnp.arange(2 * SMAX + 1, dtype=jnp.int32) - SMAX
    matches = rev_shifts[None, :, :] == lag_values[:, None, None]
    return jnp.where(matches, rev_taps[None, :, None], jnp.zeros((), jnp.bfloat16))


def correlate_kernel(own_ref, ext_ref, weight_ref, out_ref, band_ref):
    time = pl.program_id(0)
    chans = own_ref.shape[2]
    blocks = chans // BLOCK
    width = 2 * BLOCK
    for block in range(blocks):
        own = own_ref[0, :, block * BLOCK : (block + 1) * BLOCK]
        own = (own.astype(jnp.float32) * (1.0 / F)).T.astype(jnp.bfloat16)
        start = (blocks - 1 - block) * BLOCK
        for lag in range(2 * SMAX + 1):
            partner = ext_ref[time + lag, :, start : start + 3 * BLOCK]
            products = jnp.dot(own, partner, preferred_element_type=jnp.float32)
            skewed = pltpu.roll(products, 0, 1, stride=1, stride_axis=0)
            band_ref[block * BLOCK : (block + 1) * BLOCK, lag * width : (lag + 1) * width] = skewed[
                :, BLOCK:
            ].astype(jnp.bfloat16)
    total = jnp.dot(band_ref[...], weight_ref[...], preferred_element_type=jnp.float32)
    out_ref[0] = total.T


def encode_region(padded, out_times, out_chans, conv_weight, conv_bias):
    rows = padded.shape[0]
    pieces = [
        padded[:, col_off % 2, col_off // 2 : col_off // 2 + out_chans] for col_off in range(KS)
    ]
    patches = jnp.concatenate(pieces, axis=0)
    place = (
        jnp.arange(rows)[None, None, :]
        == 2 * jnp.arange(out_times)[:, None, None] + jnp.arange(KS)[None, :, None]
    ).astype(jnp.bfloat16)
    kernel = conv_weight.reshape(-1, KS, KS)
    spread = jnp.einsum("fpq,tpr->tfqr", kernel, place, preferred_element_type=jnp.float32)
    spread = spread.astype(jnp.bfloat16).reshape(-1, KS * rows)
    summed = jnp.dot(spread, patches, preferred_element_type=jnp.float32)
    summed = summed.reshape(out_times, -1, out_chans) + conv_bias[None, :, None]
    return jnp.tanh(summed).astype(jnp.bfloat16)


def body(raw_samples, channel_order, conv_weight, conv_bias, taps, shifts):
    local_times = raw_samples.shape[0] // 2
    local_chans = raw_samples.shape[1] // 2
    local_index = channel_order - lax.axis_index("chan") * raw_samples.shape[1]
    local_index = local_index.reshape(local_chans, 2).T.reshape(-1)
    ordered = jnp.take(raw_samples, local_index, axis=1).reshape(-1, 2, local_chans)
    padded = extended_2(ordered, (("chan", 2),), KS // 4)
    padded = extended_2(padded, (("tm", 0),), KS // 2)
    features = encode_region(padded, local_times, local_chans, conv_weight, conv_bias)
    extended = extended_2(features, (("chan", 2),), HALF)
    extended = extended_2(extended, (("tm", 0),), SMAX)
    extended = jnp.pad(extended, ((0, 0), (0, 0), (0, 2)))[:, :, ::-1]
    vel_count = shifts.shape[0]
    weights = lag_weights(taps, shifts).reshape(-1, vel_count)
    summed = pl.pallas_call(
        correlate_kernel,
        grid=(local_times,),
        in_specs=[
            pl.BlockSpec((1, F, local_chans), lambda t: (t, 0, 0)),
            pl.BlockSpec(extended.shape, lambda t: (0, 0, 0)),
            pl.BlockSpec(weights.shape, lambda t: (0, 0)),
        ],
        out_specs=pl.BlockSpec((1, vel_count, local_chans), lambda t: (t, 0, 0)),
        out_shape=jax.ShapeDtypeStruct((local_times, vel_count, local_chans), jnp.float32),
        scratch_shapes=[pltpu.VMEM((local_chans, weights.shape[0]), jnp.bfloat16)],
        compiler_params=pltpu.CompilerParams(vmem_limit_bytes=40 * 1024 * 1024),
    )(features, extended, weights)
    return summed.transpose(1, 0, 2)


def solution(mesh):
    placed = (P("tm", "chan"), P("chan"), P(), P(), P(), P())
    return jax.shard_map(
        body, mesh=mesh, in_specs=placed, out_specs=P(None, "tm", "chan"), check_vma=False
    )
```

```python
import jax
import jax.numpy as jnp
from jax import lax
from jax.experimental import pallas as pl
from jax.experimental.pallas import tpu as pltpu
from jax.sharding import PartitionSpec as P

F = 32
TAPS = 255
KS = 9
SMAX = 8
HALF = 127
BLOCK = 128


def extended_2(value, sides, width):
    for axis, dim in sides:
        devices, length = (lax.axis_size(axis), value.shape[dim])
        up = [(i, (i + 1) % devices) for i in range(devices - 1)]
        down = [(j, i) for i, j in up]
        last = lax.slice_in_dim(value, length - width, length, axis=dim)
        first = lax.slice_in_dim(value, 0, width, axis=dim)
        before = lax.ppermute(last, axis, up)
        after = lax.ppermute(first, axis, down)
        value = jnp.concatenate([before, value, after], axis=dim)
    return value


def lag_weights(taps, shifts):
    rev_taps = jnp.pad(taps[::-1], (1, 0))
    rev_shifts = jnp.pad(shifts.T[::-1], ((1, 0), (0, 0)))
    lag_values = jnp.arange(2 * SMAX + 1, dtype=jnp.int32) - SMAX
    matches = rev_shifts[None, :, :] == lag_values[:, None, None]
    return jnp.where(matches, rev_taps[None, :, None], jnp.zeros((), jnp.bfloat16))


def correlate_kernel(own_ref, ext_ref, weight_ref, out_ref, band_ref):
    time = pl.program_id(0)
    chans = own_ref.shape[2]
    blocks = chans // BLOCK
    width = 2 * BLOCK
    for block in range(blocks):
        own = own_ref[0, :, block * BLOCK : (block + 1) * BLOCK]
        own = (own.astype(jnp.float32) * (1.0 / F)).T.astype(jnp.bfloat16)
        start = (blocks - 1 - block) * BLOCK
        for lag in range(2 * SMAX + 1):
            partner = ext_ref[time + lag, :, start : start + 3 * BLOCK]
            products = jnp.dot(own, partner, preferred_element_type=jnp.float32)
            skewed = pltpu.roll(products, 0, 1, stride=1, stride_axis=0)
            band_ref[block * BLOCK : (block + 1) * BLOCK, lag * width : (lag + 1) * width] = skewed[
                :, BLOCK:
            ].astype(jnp.bfloat16)
    total = jnp.dot(band_ref[...], weight_ref[...], preferred_element_type=jnp.float32)
    out_ref[0] = total.T


def encode_region(padded, out_times, out_chans, conv_weight, conv_bias):
    rows = padded.shape[0]
    pieces = [
        padded[:, col_off % 2, col_off // 2 : col_off // 2 + out_chans] for col_off in range(KS)
    ]
    patches = jnp.concatenate(pieces, axis=0)
    place = (
        jnp.arange(rows)[None, None, :]
        == 2 * jnp.arange(out_times)[:, None, None] + jnp.arange(KS)[None, :, None]
    ).astype(jnp.bfloat16)
    kernel = conv_weight.reshape(-1, KS, KS)
    spread = jnp.einsum("fpq,tpr->tfqr", kernel, place, preferred_element_type=jnp.float32)
    spread = spread.astype(jnp.bfloat16).reshape(-1, KS * rows)
    summed = jnp.dot(spread, patches, preferred_element_type=jnp.float32)
    summed = summed.reshape(out_times, -1, out_chans) + conv_bias[None, :, None]
    return jnp.tanh(summed).astype(jnp.bfloat16)


def body(raw_samples, channel_order, conv_weight, conv_bias, taps, shifts):
    local_times = raw_samples.shape[0] // 2
    local_chans = raw_samples.shape[1] // 2
    local_index = channel_order - lax.axis_index("chan") * raw_samples.shape[1]
    local_index = local_index.reshape(local_chans, 2).T.reshape(-1)
    ordered = jnp.take(raw_samples, local_index, axis=1).reshape(-1, 2, local_chans)
    padded = extended_2(ordered, (("chan", 2),), HALF + KS // 4)
    padded = extended_2(padded, (("tm", 0),), 2 * SMAX + KS // 2)
    wide = local_chans + 2 * HALF
    groups = [
        encode_region(
            padded[first : first + 2 * local_times + KS - 1],
            local_times, wide, conv_weight, conv_bias,
        )
        for first in range(0, 2 * (local_times + 2 * SMAX), 2 * local_times)
    ]
    extended = jnp.concatenate(groups, axis=0)
    time_at = jnp.arange(local_times + 2 * SMAX) - SMAX + lax.axis_index("tm") * local_times
    chan_at = jnp.arange(wide) - HALF + lax.axis_index("chan") * local_chans
    time_in = (time_at >= 0) & (time_at < lax.axis_size("tm") * local_times)
    chan_in = (chan_at >= 0) & (chan_at < lax.axis_size("chan") * local_chans)
    inside = time_in[:, None, None] & chan_in[None, None, :]
    extended = jnp.where(inside, extended, jnp.zeros((), jnp.bfloat16))
    features = extended[SMAX : SMAX + local_times, :, HALF : HALF + local_chans]
    extended = jnp.pad(extended, ((0, 0), (0, 0), (0, 2)))[:, :, ::-1]
    vel_count = shifts.shape[0]
    weights = lag_weights(taps, shifts).reshape(-1, vel_count)
    summed = pl.pallas_call(
        correlate_kernel,
        grid=(local_times,),
        in_specs=[
            pl.BlockSpec((1, F, local_chans), lambda t: (t, 0, 0)),
            pl.BlockSpec(extended.shape, lambda t: (0, 0, 0)),
            pl.BlockSpec(weights.shape, lambda t: (0, 0)),
        ],
        out_specs=pl.BlockSpec((1, vel_count, local_chans), lambda t: (t, 0, 0)),
        out_shape=jax.ShapeDtypeStruct((local_times, vel_count, local_chans), jnp.float32),
        scratch_shapes=[pltpu.VMEM((local_chans, weights.shape[0]), jnp.bfloat16)],
        compiler_params=pltpu.CompilerParams(vmem_limit_bytes=40 * 1024 * 1024),
    )(features, extended, weights)
    return summed.transpose(1, 0, 2)


def solution(mesh):
    placed = (P("tm", "chan"), P("chan"), P(), P(), P(), P())
    return jax.shard_map(
        body, mesh=mesh, in_specs=placed, out_specs=P(None, "tm", "chan"), check_vma=False
    )
```

```python
import jax
import jax.numpy as jnp
from jax import lax
from jax.experimental import pallas as pl
from jax.experimental.pallas import tpu as pltpu
from jax.sharding import PartitionSpec as P

F = 32
TAPS = 255
KS = 9
SMAX = 8
HALF = 127
BLOCK = 128


def extended_2(value, sides, width):
    for axis, dim in sides:
        devices, length = (lax.axis_size(axis), value.shape[dim])
        up = [(i, (i + 1) % devices) for i in range(devices - 1)]
        down = [(j, i) for i, j in up]
        last = lax.slice_in_dim(value, length - width, length, axis=dim)
        first = lax.slice_in_dim(value, 0, width, axis=dim)
        before = lax.ppermute(last, axis, up)
        after = lax.ppermute(first, axis, down)
        value = jnp.concatenate([before, value, after], axis=dim)
    return value


def lag_weights(taps, shifts):
    rev_taps = jnp.pad(taps[::-1], (1, 0))
    rev_shifts = jnp.pad(shifts.T[::-1], ((1, 0), (0, 0)))
    lag_values = jnp.arange(2 * SMAX + 1, dtype=jnp.int32) - SMAX
    matches = rev_shifts[None, :, :] == lag_values[:, None, None]
    return jnp.where(matches, rev_taps[None, :, None], jnp.zeros((), jnp.bfloat16))


def correlate_kernel(own_ref, raw_ref, weight_ref, out_ref, band_ref, ext_ref):
    time = pl.program_id(0)

    @pl.when(time == 0)
    def _():
        rows = lax.broadcasted_iota(jnp.int32, (BLOCK, BLOCK), 0)
        cols = lax.broadcasted_iota(jnp.int32, (BLOCK, BLOCK), 1)
        flip = (rows + cols == BLOCK - 1).astype(jnp.float32).astype(jnp.bfloat16)
        times, feats, wide = raw_ref.shape
        for first in range(0, wide, BLOCK):
            part = raw_ref[:, :, first : first + BLOCK].reshape(times * feats, BLOCK)
            part = jnp.dot(part, flip, preferred_element_type=jnp.float32)
            last = wide - BLOCK - first
            ext_ref[:, :, last : last + BLOCK] = part.astype(jnp.bfloat16).reshape(times, feats, BLOCK)

    chans = own_ref.shape[2]
    blocks = chans // BLOCK
    width = 2 * BLOCK
    for block in range(blocks):
        own = own_ref[0, :, block * BLOCK : (block + 1) * BLOCK]
        own = (own.astype(jnp.float32) * (1.0 / F)).T.astype(jnp.bfloat16)
        start = (blocks - 1 - block) * BLOCK
        for lag in range(2 * SMAX + 1):
            partner = ext_ref[time + lag, :, start : start + 3 * BLOCK]
            products = jnp.dot(own, partner, preferred_element_type=jnp.float32)
            skewed = pltpu.roll(products, 0, 1, stride=1, stride_axis=0)
            band_ref[block * BLOCK : (block + 1) * BLOCK, lag * width : (lag + 1) * width] = skewed[
                :, BLOCK:
            ].astype(jnp.bfloat16)
    total = jnp.dot(band_ref[...], weight_ref[...], preferred_element_type=jnp.float32)
    out_ref[0] = total.T


def encode_region(padded, out_times, out_chans, conv_weight, conv_bias):
    rows = padded.shape[0]
    pieces = [
        padded[:, col_off % 2, col_off // 2 : col_off // 2 + out_chans] for col_off in range(KS)
    ]
    patches = jnp.concatenate(pieces, axis=0)
    place = (
        jnp.arange(rows)[None, None, :]
        == 2 * jnp.arange(out_times)[:, None, None] + jnp.arange(KS)[None, :, None]
    ).astype(jnp.bfloat16)
    kernel = conv_weight.reshape(-1, KS, KS)
    spread = jnp.einsum("fpq,tpr->tfqr", kernel, place, preferred_element_type=jnp.float32)
    spread = spread.astype(jnp.bfloat16).reshape(-1, KS * rows)
    summed = jnp.dot(spread, patches, preferred_element_type=jnp.float32)
    summed = summed.reshape(out_times, -1, out_chans) + conv_bias[None, :, None]
    return jnp.tanh(summed).astype(jnp.bfloat16)


def body(raw_samples, channel_order, conv_weight, conv_bias, taps, shifts):
    local_times = raw_samples.shape[0] // 2
    local_chans = raw_samples.shape[1] // 2
    local_index = channel_order - lax.axis_index("chan") * raw_samples.shape[1]
    local_index = local_index.reshape(local_chans, 2).T.reshape(-1)
    ordered = jnp.take(raw_samples, local_index, axis=1).reshape(-1, 2, local_chans)
    padded = extended_2(ordered, (("chan", 2),), HALF + KS // 4)
    padded = extended_2(padded, (("tm", 0),), 2 * SMAX + KS // 2)
    wide = local_chans + 2 * HALF
    groups = [
        encode_region(
            padded[first : first + 2 * local_times + KS - 1],
            local_times, wide, conv_weight, conv_bias,
        )
        for first in range(0, 2 * (local_times + 2 * SMAX), 2 * local_times)
    ]
    extended = jnp.concatenate(groups, axis=0)
    time_at = jnp.arange(local_times + 2 * SMAX) - SMAX + lax.axis_index("tm") * local_times
    chan_at = jnp.arange(wide) - HALF + lax.axis_index("chan") * local_chans
    time_in = (time_at >= 0) & (time_at < lax.axis_size("tm") * local_times)
    chan_in = (chan_at >= 0) & (chan_at < lax.axis_size("chan") * local_chans)
    inside = time_in[:, None, None] & chan_in[None, None, :]
    extended = jnp.where(inside, extended, jnp.zeros((), jnp.bfloat16))
    features = extended[SMAX : SMAX + local_times, :, HALF : HALF + local_chans]
    extended = jnp.pad(extended, ((0, 0), (0, 0), (0, 2)))
    vel_count = shifts.shape[0]
    weights = lag_weights(taps, shifts).reshape(-1, vel_count)
    summed = pl.pallas_call(
        correlate_kernel,
        grid=(local_times,),
        in_specs=[
            pl.BlockSpec((1, F, local_chans), lambda t: (t, 0, 0)),
            pl.BlockSpec(extended.shape, lambda t: (0, 0, 0)),
            pl.BlockSpec(weights.shape, lambda t: (0, 0)),
        ],
        out_specs=pl.BlockSpec((1, vel_count, local_chans), lambda t: (t, 0, 0)),
        out_shape=jax.ShapeDtypeStruct((local_times, vel_count, local_chans), jnp.float32),
        scratch_shapes=[
            pltpu.VMEM((local_chans, weights.shape[0]), jnp.bfloat16),
            pltpu.VMEM(extended.shape, jnp.bfloat16),
        ],
        compiler_params=pltpu.CompilerParams(vmem_limit_bytes=40 * 1024 * 1024),
    )(features, extended, weights)
    return summed.transpose(1, 0, 2)


def solution(mesh):
    placed = (P("tm", "chan"), P("chan"), P(), P(), P(), P())
    return jax.shard_map(
        body, mesh=mesh, in_specs=placed, out_specs=P(None, "tm", "chan"), check_vma=False
    )
```

```python
import jax
import jax.numpy as jnp
from jax import lax
from jax.experimental import pallas as pl
from jax.experimental.pallas import tpu as pltpu
from jax.sharding import PartitionSpec as P

F = 32
TAPS = 255
KS = 9
SMAX = 8
HALF = 127
BLOCK = 128


def extended_2(value, sides, width):
    for axis, dim in sides:
        devices, length = (lax.axis_size(axis), value.shape[dim])
        up = [(i, (i + 1) % devices) for i in range(devices - 1)]
        down = [(j, i) for i, j in up]
        last = lax.slice_in_dim(value, length - width, length, axis=dim)
        first = lax.slice_in_dim(value, 0, width, axis=dim)
        before = lax.ppermute(last, axis, up)
        after = lax.ppermute(first, axis, down)
        value = jnp.concatenate([before, value, after], axis=dim)
    return value


def lag_weights(taps, shifts):
    rev_taps = jnp.pad(taps[::-1], (1, 0))
    rev_shifts = jnp.pad(shifts.T[::-1], ((1, 0), (0, 0)))
    lag_values = jnp.arange(2 * SMAX + 1, dtype=jnp.int32) - SMAX
    matches = rev_shifts[None, :, :] == lag_values[:, None, None]
    return jnp.where(matches, rev_taps[None, :, None], jnp.zeros((), jnp.bfloat16))


def correlate_kernel(own_ref, raw_ref, weight_ref, out_ref, band_ref, ext_ref):
    time = pl.program_id(0)

    @pl.when(time == 0)
    def _():
        rows = lax.broadcasted_iota(jnp.int32, (BLOCK, BLOCK), 0)
        cols = lax.broadcasted_iota(jnp.int32, (BLOCK, BLOCK), 1)
        flip = (rows + cols == BLOCK - 1).astype(jnp.float32).astype(jnp.bfloat16)
        times, feats, wide = raw_ref.shape
        for first in range(0, wide, BLOCK):
            part = raw_ref[:, :, first : first + BLOCK].reshape(times * feats, BLOCK)
            part = jnp.dot(part, flip, preferred_element_type=jnp.float32)
            last = wide - BLOCK - first
            ext_ref[:, :, last : last + BLOCK] = part.astype(jnp.bfloat16).reshape(times, feats, BLOCK)

    chans = own_ref.shape[2]
    blocks = chans // BLOCK
    width = 2 * BLOCK
    owns = []
    for block in range(blocks):
        own = own_ref[0, :, block * BLOCK : (block + 1) * BLOCK]
        owns.append((own.astype(jnp.float32) * (1.0 / F)).T.astype(jnp.bfloat16))
    for lag in range(2 * SMAX + 1):
        for block in range(blocks):
            start = (blocks - 1 - block) * BLOCK
            partner = ext_ref[time + lag, :, start : start + 3 * BLOCK]
            products = jnp.dot(owns[block], partner, preferred_element_type=jnp.float32)
            skewed = pltpu.roll(products, 0, 1, stride=1, stride_axis=0)
            band_ref[block * BLOCK : (block + 1) * BLOCK, lag * width : (lag + 1) * width] = skewed[
                :, BLOCK:
            ].astype(jnp.bfloat16)
    total = jnp.dot(band_ref[...], weight_ref[...], preferred_element_type=jnp.float32)
    out_ref[0] = total.T


def encode_region(padded, out_times, out_chans, conv_weight, conv_bias):
    rows = padded.shape[0]
    pieces = [
        padded[:, col_off % 2, col_off // 2 : col_off // 2 + out_chans] for col_off in range(KS)
    ]
    patches = jnp.concatenate(pieces, axis=0)
    place = (
        jnp.arange(rows)[None, None, :]
        == 2 * jnp.arange(out_times)[:, None, None] + jnp.arange(KS)[None, :, None]
    ).astype(jnp.bfloat16)
    kernel = conv_weight.reshape(-1, KS, KS)
    spread = jnp.einsum("fpq,tpr->tfqr", kernel, place, preferred_element_type=jnp.float32)
    spread = spread.astype(jnp.bfloat16).reshape(-1, KS * rows)
    summed = jnp.dot(spread, patches, preferred_element_type=jnp.float32)
    summed = summed.reshape(out_times, -1, out_chans) + conv_bias[None, :, None]
    return jnp.tanh(summed).astype(jnp.bfloat16)


def body(raw_samples, channel_order, conv_weight, conv_bias, taps, shifts):
    local_times = raw_samples.shape[0] // 2
    local_chans = raw_samples.shape[1] // 2
    local_index = channel_order - lax.axis_index("chan") * raw_samples.shape[1]
    local_index = local_index.reshape(local_chans, 2).T.reshape(-1)
    ordered = jnp.take(raw_samples, local_index, axis=1).reshape(-1, 2, local_chans)
    padded = extended_2(ordered, (("chan", 2),), HALF + KS // 4)
    padded = extended_2(padded, (("tm", 0),), 2 * SMAX + KS // 2)
    wide = local_chans + 2 * HALF
    groups = [
        encode_region(
            padded[first : first + 2 * local_times + KS - 1],
            local_times, wide, conv_weight, conv_bias,
        )
        for first in range(0, 2 * (local_times + 2 * SMAX), 2 * local_times)
    ]
    extended = jnp.concatenate(groups, axis=0)
    time_at = jnp.arange(local_times + 2 * SMAX) - SMAX + lax.axis_index("tm") * local_times
    chan_at = jnp.arange(wide) - HALF + lax.axis_index("chan") * local_chans
    time_in = (time_at >= 0) & (time_at < lax.axis_size("tm") * local_times)
    chan_in = (chan_at >= 0) & (chan_at < lax.axis_size("chan") * local_chans)
    inside = time_in[:, None, None] & chan_in[None, None, :]
    extended = jnp.where(inside, extended, jnp.zeros((), jnp.bfloat16))
    features = extended[SMAX : SMAX + local_times, :, HALF : HALF + local_chans]
    extended = jnp.pad(extended, ((0, 0), (0, 0), (0, 2)))
    vel_count = shifts.shape[0]
    weights = lag_weights(taps, shifts).reshape(-1, vel_count)
    summed = pl.pallas_call(
        correlate_kernel,
        grid=(local_times,),
        in_specs=[
            pl.BlockSpec((1, F, local_chans), lambda t: (t, 0, 0)),
            pl.BlockSpec(extended.shape, lambda t: (0, 0, 0)),
            pl.BlockSpec(weights.shape, lambda t: (0, 0)),
        ],
        out_specs=pl.BlockSpec((1, vel_count, local_chans), lambda t: (t, 0, 0)),
        out_shape=jax.ShapeDtypeStruct((local_times, vel_count, local_chans), jnp.float32),
        scratch_shapes=[
            pltpu.VMEM((local_chans, weights.shape[0]), jnp.bfloat16),
            pltpu.VMEM(extended.shape, jnp.bfloat16),
        ],
        compiler_params=pltpu.CompilerParams(vmem_limit_bytes=40 * 1024 * 1024),
    )(features, extended, weights)
    return summed.transpose(1, 0, 2)


def solution(mesh):
    placed = (P("tm", "chan"), P("chan"), P(), P(), P(), P())
    return jax.shard_map(
        body, mesh=mesh, in_specs=placed, out_specs=P(None, "tm", "chan"), check_vma=False
    )
```
